32 devices in a mesh: win: 2 (over y), row: 4 (over z), col: 4 (over x, core).
Axes of the slice: x: 2, y: 2, z: 4, core: 2. Of those that a mesh axis runs over, the one named last changes fastest.
Arguments:
- records: bfloat16 [32, 4096, 1024], P('win', ('row', 'col'))
- tile_pairs: int32 [4, 4, 4, 2], P('row', 'col'), may hold values from 0 to 3
- tile_count: int32 [4, 4], P('row', 'col'), may hold values from 1 to 4, as said below
- bin_index: int32 [32], replicated, may hold values from 1 to 511, as said below
Outputs:
- cross_tiles: bfloat16 [4, 4, 4, 2, 32, 256, 256], P('row', 'col', 'win')
The draws below stay inside these ranges and needn't reach their ends.
Inputs may be any that keep to these rules, and one draw needn't show every extreme that they name: Slots 0 to tile_count - 1 of a cell are live; some cell has all 4 live and some cell one. `bin_index`: distinct and increasing; the first is 1 and the last 511.
All inputs are finite; a program needn't handle non-finite values.
Results may differ from the reference program's by a relative error of at most 0.0069.
Values may be sent and summed in bfloat16 or wider, within the bound.
A program may use at most 256 MiB of HBM per device.

```python
import math
import jax
import jax.numpy as jnp
from jax import lax

CHAN_BLOCK = 256
SAMPLES = 1024
KEPT_BINS = 32
SLOTS = 4
GRID_SIDE = 4
WINDOWS = 32
CHANNELS = 4096


def draw_records(key, part):
    keys = jax.random.split(key, 3)
    noise = jax.random.normal(keys[0], (WINDOWS, CHANNELS, SAMPLES), jnp.float32)
    spread = math.log(10.0)
    window_scale = jnp.exp(jax.random.uniform(keys[1], (WINDOWS, 1, 1), jnp.float32, 0.0, spread))
    channel_scale = jnp.exp(jax.random.uniform(keys[2], (1, CHANNELS, 1), jnp.float32, 0.0, spread))
    return (noise * window_scale * channel_scale).astype(jnp.bfloat16)


def draw_tile_count(key, part):
    keys = jax.random.split(key, 3)
    cells = GRID_SIDE * GRID_SIDE
    counts = jax.random.randint(keys[0], (cells,), 1, SLOTS + 1, dtype=jnp.int32)
    highest = jax.random.randint(keys[1], (), 0, cells, dtype=jnp.int32)
    lowest = (highest + 1 + jax.random.randint(keys[2], (), 0, cells - 1, dtype=jnp.int32)) % cells
    counts = counts.at[highest].set(SLOTS)
    counts = counts.at[lowest].set(1)
    return counts.reshape(GRID_SIDE, GRID_SIDE).astype(jnp.int32)


def draw_bin_index(key, part):
    inner = jax.random.permutation(key, SAMPLES // 2 - 3)[:KEPT_BINS - 2].astype(jnp.int32) + 2
    inner = jnp.sort(inner)
    first = jnp.ones((1,), jnp.int32)
    final = jnp.full((1,), SAMPLES // 2 - 1, jnp.int32)
    return jnp.concatenate([first, inner, final]).astype(jnp.int32)


def plant(result, rng, smallest, top_value):
    shape = result.shape
    place = [jax.random.randint(jax.random.fold_in(rng, axis), (), 0, shape[axis]) for axis in range(len(shape))]
    result = result.at[tuple(place)].set(smallest)
    longest = shape.index(max(shape))
    place[longest] = (place[longest] + 1) % shape[longest]
    return result.at[tuple(place)].set(top_value)


def setup_inputs(seed: int = 0) -> dict:
    key_list = jax.random.split(jax.random.key(seed), 5)
    records = draw_records(jax.random.fold_in(key_list[4], 71), 0)
    tile_pairs = plant(jax.random.randint(key_list[1], (GRID_SIDE, GRID_SIDE, SLOTS, 2), 0, GRID_SIDE), jax.random.fold_in(key_list[1], 1), 0, GRID_SIDE - 1).astype(jnp.int32)
    tile_count = draw_tile_count(jax.random.fold_in(key_list[4], 71), 0)
    bin_index = draw_bin_index(jax.random.fold_in(key_list[4], 71), 0)
    return {"records": records, "tile_pairs": tile_pairs, "tile_count": tile_count, "bin_index": bin_index}


def dft_table(bin_index, length):
    sample_ids = jnp.arange(length, dtype=jnp.int32)
    phases = sample_ids[:, None] * bin_index[None, :] % length
    angles = 2.0 * math.pi / length * phases.astype(jnp.float32)
    window_taper = 0.5 - 0.5 * jnp.cos(2.0 * math.pi / length * sample_ids.astype(jnp.float32))
    cosine = window_taper[:, None] * jnp.cos(angles)
    sine = -window_taper[:, None] * jnp.sin(angles)
    return jnp.concatenate([cosine, sine], axis=1).astype(jnp.bfloat16)

def reference(records, tile_pairs, tile_count, bin_index):
    phase_table = dft_table(bin_index, SAMPLES)

    def whiten_window(window_rows):
        spectrum = jnp.dot(window_rows, phase_table, preferred_element_type=jnp.float32)
        energy = jnp.sqrt(lax.optimization_barrier(jnp.mean(spectrum * spectrum, axis=1, keepdims=True)) + 1e-06)
        return (spectrum / energy).astype(jnp.bfloat16)
    whitened = lax.map(whiten_window, records)
    blocks = whitened.reshape(WINDOWS, GRID_SIDE * GRID_SIDE, CHAN_BLOCK, 2, KEPT_BINS)
    flat_pairs = tile_pairs.reshape(GRID_SIDE * GRID_SIDE * SLOTS, 2).astype(jnp.int32)
    flat_count = tile_count.reshape(GRID_SIDE * GRID_SIDE).astype(jnp.int32)
    item_ids = jnp.arange(GRID_SIDE * GRID_SIDE * SLOTS, dtype=jnp.int32)

    def one_tile(item):
        cell = item // SLOTS
        slot = item % SLOTS
        grid_row = cell // GRID_SIDE
        grid_col = cell % GRID_SIDE
        first_id = grid_row * GRID_SIDE + flat_pairs[item, 0]
        second_id = flat_pairs[item, 1] * GRID_SIDE + grid_col
        first_block = blocks[:, first_id].astype(jnp.float32)
        second_block = blocks[:, second_id].astype(jnp.float32)
        first_real = first_block[:, :, 0]
        first_imag = first_block[:, :, 1]
        second_real = second_block[:, :, 0]
        second_imag = second_block[:, :, 1]
        real_part = jnp.einsum('wpk,wqk->kpq', first_real, second_real) + jnp.einsum('wpk,wqk->kpq', first_imag, second_imag)
        imag_part = jnp.einsum('wpk,wqk->kpq', first_imag, second_real) - jnp.einsum('wpk,wqk->kpq', first_real, second_imag)
        live = (slot < flat_count[cell]).astype(jnp.float32)
        return (jnp.stack([real_part, imag_part]) * live).astype(jnp.bfloat16)
    tiles = lax.map(one_tile, item_ids)
    return tiles.reshape(GRID_SIDE, GRID_SIDE, SLOTS, 2, KEPT_BINS, CHAN_BLOCK, CHAN_BLOCK)
```

```python
import functools
import math

import jax
import jax.numpy as jnp
from jax import lax
from jax.experimental import pallas as pl
from jax.experimental.pallas import tpu as pltpu
from jax.sharding import PartitionSpec as P

GROUP = 8
UP, DOWN, PARTNER, RIGHT, LEFT, SIBLING = range(6)


def dft_table(bin_index, length):
    sample_ids = jnp.arange(length, dtype=jnp.int32)
    phases = sample_ids[:, None] * bin_index[None, :] % length
    angles = 2.0 * math.pi / length * phases.astype(jnp.float32)
    window_taper = 0.5 - 0.5 * jnp.cos(2.0 * math.pi / length * sample_ids.astype(jnp.float32))
    cosine = window_taper[:, None] * jnp.cos(angles)
    sine = -window_taper[:, None] * jnp.sin(angles)
    table = jnp.stack([cosine, sine], axis=2).astype(jnp.bfloat16)
    return table.reshape(length, -1).T


def gather_kernel(rows, cols, groups, rec_hbm, basis_ref, sets, rec, spec, own,
                  rec_sem, local_sem, send_sem, recv_sem):
    w, r, q = lax.axis_index("win"), lax.axis_index("row"), lax.axis_index("col")
    chips = cols // 2
    x = q // 2
    other = 1 - w
    sib = q + 1 - 2 * (q % 2)
    mine, theirs = w * groups, other * groups
    device = {
        UP: (w, r + 1, q), DOWN: (w, r - 1, q), PARTNER: (other, r, q),
        RIGHT: (w, r, q + 2), LEFT: (w, r, q - 2), SIBLING: (w, r, sib),
    }
    exists = {
        UP: r < rows - 1, DOWN: r > 0, PARTNER: None,
        RIGHT: x < chips - 1, LEFT: x > 0, SIBLING: None,
    }

    def fetch(i):
        part = pl.ds(i * GROUP, GROUP)
        return pltpu.make_async_copy(rec_hbm.at[part], rec.at[part], rec_sem.at[i])

    for i in range(groups):
        fetch(i).start()

    def guarded(way, f):
        if exists[way] is None:
            f()
        else:
            pl.when(exists[way])(f)

    barrier = pltpu.get_barrier_semaphore()
    for way in range(6):
        guarded(way, lambda way=way: pl.semaphore_signal(
            barrier, inc=1, device_id=device[way], device_id_type=pl.DeviceIdType.MESH))
    ends = sum(exists[way].astype(jnp.int32) for way in (UP, DOWN, RIGHT, LEFT))
    pl.semaphore_wait(barrier, 2 + ends)

    def copy(way, src, slot, g):
        return pltpu.make_async_remote_copy(
            src_ref=src, dst_ref=sets.at[slot, g], send_sem=send_sem.at[way, slot, g],
            recv_sem=recv_sem.at[slot, g], device_id=device[way],
            device_id_type=pl.DeviceIdType.MESH)

    pending = []

    def send(way, src, slot, g, cond=None):
        def go():
            guarded(way, lambda: copy(way, src, slot, g).start())

        def done():
            guarded(way, lambda: copy(way, src, slot, g).wait_send())

        if cond is None:
            go()
        pending.append((cond, done))
        return go

    def arrived(slot, g):
        copy(PARTNER, sets.at[slot, g], slot, g).wait_recv()

    keeps = []
    for i in range(groups):
        fetch(i).wait()

        def one_window(v, _, i=i):
            s = lax.dot_general(basis_ref[...], rec[i * GROUP + v], (((1,), (1,)), ((), ())),
                                preferred_element_type=jnp.float32)
            scale = 1.0 / jnp.sqrt(jnp.mean(s * s, axis=0, keepdims=True) + 1e-06)
            s = s * scale
            for lane in range(spec.shape[0]):
                spec[lane, pl.ds(v, s.shape[0], stride=GROUP), :] = s[:, lane * 128:(lane + 1) * 128]
            return 0

        lax.fori_loop(0, GROUP, one_window, 0)
        for lane in range(spec.shape[0]):
            own[i, :, :, lane * 128:(lane + 1) * 128] = spec[lane].astype(jnp.bfloat16).reshape(
                own.shape[1], own.shape[2], 128)
        for way in (PARTNER, UP, DOWN):
            send(way, own.at[i], r, mine + i)
        for way in (RIGHT, LEFT, SIBLING):
            send(way, own.at[i], rows + q, mine + i)
        keep = pltpu.make_async_copy(own.at[i], sets.at[r, mine + i], local_sem.at[i])
        keep.start()
        keeps.append(keep)

    def relay(cond, slot, g, ways):
        goes = [send(way, sets.at[slot, g], slot, g, cond) for way in ways]

        def go():
            arrived(slot, g)
            for f in goes:
                f()

        pl.when(cond)(go)

    def along_x(g):
        for d in range(1, chips):
            relay(x - d >= 0, rows + q - 2 * d, g, (RIGHT, SIBLING))
            relay(x + d < chips, rows + q + 2 * d, g, (LEFT, SIBLING))

    for h in range(1, rows):
        for i in range(groups):
            if h == 1:
                arrived(r, theirs + i)
                for way in (RIGHT, LEFT, SIBLING):
                    send(way, sets.at[r, theirs + i], rows + q, theirs + i)
            relay(r - h >= 0, r - h, mine + i, (UP, PARTNER))
            relay(r + h < rows, r + h, mine + i, (DOWN, PARTNER))
        if h == 1:
            for i in range(groups):
                along_x(mine + i)
    for i in range(groups):
        along_x(theirs + i)

    for h in range(1, rows):
        for i in range(groups):
            pl.when(r - h >= 0)(lambda h=h, i=i: arrived(r - h, theirs + i))
            pl.when(r + h < rows)(lambda h=h, i=i: arrived(r + h, theirs + i))
    for c in range(chips):
        for g in range(2 * groups):
            arrived(rows + 2 * c + 1 - q % 2, g)
    for keep in keeps:
        keep.wait()
    for cond, done in pending:
        if cond is None:
            done()
        else:
            pl.when(cond)(done)


def gather(records, table, rows, cols):
    windows, channels, length = records.shape
    groups = windows // GROUP
    entries = table.shape[0]
    bins = entries // 2
    slots = rows + cols
    return pl.pallas_call(
        functools.partial(gather_kernel, rows, cols, groups),
        out_shape=jax.ShapeDtypeStruct(
            (slots, 2 * groups, bins, 2 * GROUP, channels), jnp.bfloat16),
        in_specs=[pl.BlockSpec(memory_space=pl.ANY), pl.BlockSpec(memory_space=pltpu.VMEM)],
        out_specs=pl.BlockSpec(memory_space=pl.ANY),
        scratch_shapes=[
            pltpu.VMEM(records.shape, jnp.bfloat16),
            pltpu.VMEM((channels // 128, entries * GROUP, 128), jnp.float32),
            pltpu.VMEM((groups, bins, 2 * GROUP, channels), jnp.bfloat16),
            pltpu.SemaphoreType.DMA((groups,)),
            pltpu.SemaphoreType.DMA((groups,)),
            pltpu.SemaphoreType.DMA((6, slots, 2 * groups)),
            pltpu.SemaphoreType.DMA((slots, 2 * groups)),
        ],
        compiler_params=pltpu.CompilerParams(
            collective_id=0, has_side_effects=True, vmem_limit_bytes=40 * 2**20),
        cost_estimate=pl.CostEstimate(
            flops=2 * windows * channels * length * entries,
            bytes_accessed=windows * channels * length * 2, transcendentals=0),
    )(records, table)


def cross_kernel(picks, first, second, out):
    slot = pl.program_id(0)
    live = picks[slot, 2] != 0

    @pl.when(live)
    def _():
        for k in range(first.shape[2]):
            a = first[0, :, k].reshape(-1, first.shape[4])
            b = second[0, :, k].reshape(a.shape)
            parts = b.astype(jnp.float32).reshape(first.shape[1], 2, GROUP, a.shape[1])
            turned = jnp.concatenate([-parts[:, 1:], parts[:, :1]], axis=1)
            turned = turned.reshape(a.shape).astype(jnp.bfloat16)
            for e, m in enumerate((b, turned)):
                out[0, 0, 0, e, k] = lax.dot_general(
                    a, m, (((0,), (0,)), ((), ())), preferred_element_type=jnp.float32
                ).astype(jnp.bfloat16)

    @pl.when(jnp.logical_not(live))
    def _():
        out[...] = jnp.zeros_like(out)


def cross(sets, picks):
    _, groups, bins, pairs, channels = sets.shape
    owned = picks.shape[0]
    step = math.gcd(bins, 4)
    block = (1, groups, step, pairs, channels)
    return pl.pallas_call(
        cross_kernel,
        out_shape=jax.ShapeDtypeStruct(
            (1, 1, owned, 2, bins, channels, channels), jnp.bfloat16),
        grid_spec=pltpu.PrefetchScalarGridSpec(
            num_scalar_prefetch=1,
            grid=(owned, bins // step),
            in_specs=[
                pl.BlockSpec(block, lambda s, k, p: (p[s, 0], 0, k, 0, 0)),
                pl.BlockSpec(block, lambda s, k, p: (p[s, 1], 0, k, 0, 0)),
            ],
            out_specs=pl.BlockSpec(
                (1, 1, 1, 2, step, channels, channels), lambda s, k, p: (0, 0, s, 0, k, 0, 0)),
        ),
        compiler_params=pltpu.CompilerParams(vmem_limit_bytes=40 * 2**20),
        cost_estimate=pl.CostEstimate(
            flops=4 * owned * bins * channels * channels * groups * pairs,
            bytes_accessed=4 * owned * bins * channels * channels, transcendentals=0),
    )(picks, sets, sets)


def body(records, tile_pairs, tile_count, bin_index):
    rows, cols = lax.axis_size("row"), lax.axis_size("col")
    r, q = lax.axis_index("row"), lax.axis_index("col")
    table = dft_table(bin_index, records.shape[2])
    sets = gather(records, table, rows, cols)
    owned = tile_pairs.shape[2] // lax.axis_size("win")
    begin = lax.axis_index("win") * owned
    chosen = lax.dynamic_slice_in_dim(tile_pairs[0, 0], begin, owned, 0)
    live = (begin + jnp.arange(owned, dtype=jnp.int32) < tile_count[0, 0]).astype(jnp.int32)
    first = jnp.where(chosen[:, 0] == q, r, rows + chosen[:, 0])
    picks = jnp.stack([first, chosen[:, 1], live], axis=1).astype(jnp.int32)
    return cross(sets, picks)


def solution(mesh):
    return jax.shard_map(
        body,
        mesh=mesh,
        in_specs=(
            P("win", ("row", "col"), None),
            P("row", "col", None, None),
            P("row", "col"),
            P(),
        ),
        out_specs=P("row", "col", "win", None, None, None, None),
        check_vma=False,
    )
```

```python
import functools
import math

import jax
import jax.numpy as jnp
from jax import lax
from jax.experimental import pallas as pl
from jax.experimental.pallas import tpu as pltpu
from jax.sharding import PartitionSpec as P

GROUP = 8
UP, DOWN, PARTNER, RIGHT, LEFT, SIBLING = range(6)


def dft_tables(bin_index, length):
    sample_ids = jnp.arange(length, dtype=jnp.int32)
    phases = bin_index[:, None] * sample_ids[None, :] % length
    angles = 2.0 * math.pi / length * phases.astype(jnp.float32)
    window_taper = 0.5 - 0.5 * jnp.cos(2.0 * math.pi / length * sample_ids.astype(jnp.float32))
    cosine = window_taper[None, :] * jnp.cos(angles)
    sine = -window_taper[None, :] * jnp.sin(angles)
    return cosine.astype(jnp.bfloat16), sine.astype(jnp.bfloat16)


def gather_kernel(rows, cols, groups, rec_hbm, cos_ref, sin_ref, sets, rec, spec, own,
                  rec_sem, local_sem, send_sem, recv_sem):
    w, r, q = lax.axis_index("win"), lax.axis_index("row"), lax.axis_index("col")
    chips = cols // 2
    x = q // 2
    other = 1 - w
    sib = q + 1 - 2 * (q % 2)
    mine, theirs = w * groups, other * groups
    device = {
        UP: (w, r + 1, q), DOWN: (w, r - 1, q), PARTNER: (other, r, q),
        RIGHT: (w, r, q + 2), LEFT: (w, r, q - 2), SIBLING: (w, r, sib),
    }
    exists = {
        UP: r < rows - 1, DOWN: r > 0, PARTNER: None,
        RIGHT: x < chips - 1, LEFT: x > 0, SIBLING: None,
    }

    def fetch(i):
        part = pl.ds(i * GROUP, GROUP)
        return pltpu.make_async_copy(rec_hbm.at[part], rec.at[part], rec_sem.at[i])

    for i in range(groups):
        fetch(i).start()

    def guarded(way, f):
        if exists[way] is None:
            f()
        else:
            pl.when(exists[way])(f)

    barrier = pltpu.get_barrier_semaphore()
    for way in range(6):
        guarded(way, lambda way=way: pl.semaphore_signal(
            barrier, inc=1, device_id=device[way], device_id_type=pl.DeviceIdType.MESH))
    ends = sum(exists[way].astype(jnp.int32) for way in (UP, DOWN, RIGHT, LEFT))
    pl.semaphore_wait(barrier, 2 + ends)

    def copy(way, src, slot, g):
        return pltpu.make_async_remote_copy(
            src_ref=src, dst_ref=sets.at[slot, g], send_sem=send_sem.at[way, slot, g],
            recv_sem=recv_sem.at[slot, g], device_id=device[way],
            device_id_type=pl.DeviceIdType.MESH)

    pending = []

    def send(way, src, slot, g, cond=None):
        def go():
            guarded(way, lambda: copy(way, src, slot, g).start())

        def done():
            guarded(way, lambda: copy(way, src, slot, g).wait_send())

        if cond is None:
            go()
        pending.append((cond, done))
        return go

    def arrived(slot, g):
        copy(PARTNER, sets.at[slot, g], slot, g).wait_recv()

    bins = cos_ref.shape[0]
    keeps = []
    for i in range(groups):
        fetch(i).wait()

        def one_window(v, _, i=i):
            table = jnp.concatenate([cos_ref[...], sin_ref[...]], axis=0)
            s = lax.dot_general(table, rec[i * GROUP + v], (((1,), (1,)), ((), ())),
                                preferred_element_type=jnp.float32)
            scale = 1.0 / jnp.sqrt(jnp.mean(s * s, axis=0, keepdims=True) + 1e-06)
            s = s * scale
            for lane in range(spec.shape[0]):
                part = s[:, lane * 128:(lane + 1) * 128]
                spec[lane, pl.ds(v, bins, stride=2 * GROUP), :] = part[:bins]
                spec[lane, pl.ds(v + GROUP, bins, stride=2 * GROUP), :] = part[bins:]
            return 0

        lax.fori_loop(0, GROUP, one_window, 0)
        for lane in range(spec.shape[0]):
            own[i, :, :, lane * 128:(lane + 1) * 128] = spec[lane].astype(jnp.bfloat16).reshape(
                own.shape[1], own.shape[2], 128)
        for way in (PARTNER, UP, DOWN):
            send(way, own.at[i], r, mine + i)
        for way in (RIGHT, LEFT, SIBLING):
            send(way, own.at[i], rows + q, mine + i)
        keep = pltpu.make_async_copy(own.at[i], sets.at[r, mine + i], local_sem.at[i])
        keep.start()
        keeps.append(keep)

    def relay(cond, slot, g, ways):
        goes = [send(way, sets.at[slot, g], slot, g, cond) for way in ways]

        def go():
            arrived(slot, g)
            for f in goes:
                f()

        pl.when(cond)(go)

    def along_x(g):
        for d in range(1, chips):
            relay(x - d >= 0, rows + q - 2 * d, g, (RIGHT, SIBLING))
            relay(x + d < chips, rows + q + 2 * d, g, (LEFT, SIBLING))

    for h in range(1, rows):
        for i in range(groups):
            if h == 1:
                arrived(r, theirs + i)
                for way in (RIGHT, LEFT, SIBLING):
                    send(way, sets.at[r, theirs + i], rows + q, theirs + i)
                if i == groups - 1:
                    for way in (UP, DOWN):
                        send(way, sets.at[r, theirs + i], r, theirs + i)
            shared = () if h == 1 and i == groups - 1 else (PARTNER,)
            relay(r - h >= 0, r - h, mine + i, (UP,) + shared)
            relay(r + h < rows, r + h, mine + i, (DOWN,) + shared)
        if h == 1:
            for i in range(groups):
                along_x(mine + i)
    for i in range(groups):
        along_x(theirs + i)

    for h in range(1, rows):
        for i in range(groups):
            pl.when(r - h >= 0)(lambda h=h, i=i: arrived(r - h, theirs + i))
            pl.when(r + h < rows)(lambda h=h, i=i: arrived(r + h, theirs + i))
    for c in range(chips):
        for g in range(2 * groups):
            arrived(rows + 2 * c + 1 - q % 2, g)
    for keep in keeps:
        keep.wait()
    for cond, done in pending:
        if cond is None:
            done()
        else:
            pl.when(cond)(done)


def gather(records, tables, rows, cols):
    windows, channels, length = records.shape
    groups = windows // GROUP
    entries = 2 * tables[0].shape[0]
    bins = entries // 2
    slots = rows + cols
    return pl.pallas_call(
        functools.partial(gather_kernel, rows, cols, groups),
        out_shape=jax.ShapeDtypeStruct(
            (slots, 2 * groups, bins, 2 * GROUP, channels), jnp.bfloat16),
        in_specs=[pl.BlockSpec(memory_space=pl.ANY)] + [pl.BlockSpec(memory_space=pltpu.VMEM)] * 2,
        out_specs=pl.BlockSpec(memory_space=pl.ANY),
        scratch_shapes=[
            pltpu.VMEM(records.shape, jnp.bfloat16),
            pltpu.VMEM((channels // 128, entries * GROUP, 128), jnp.float32),
            pltpu.VMEM((groups, bins, 2 * GROUP, channels), jnp.bfloat16),
            pltpu.SemaphoreType.DMA((groups,)),
            pltpu.SemaphoreType.DMA((groups,)),
            pltpu.SemaphoreType.DMA((6, slots, 2 * groups)),
            pltpu.SemaphoreType.DMA((slots, 2 * groups)),
        ],
        compiler_params=pltpu.CompilerParams(
            collective_id=0, has_side_effects=True, vmem_limit_bytes=40 * 2**20),
        cost_estimate=pl.CostEstimate(
            flops=2 * windows * channels * length * entries,
            bytes_accessed=windows * channels * length * 2, transcendentals=0),
    )(records, *tables)


def cross_kernel(pairs, count, place, first, second, out):
    live = place[0] + pl.program_id(0) < count[0]

    @pl.when(live)
    def _():
        for k in range(first.shape[2]):
            a = first[0, :, k].reshape(-1, first.shape[4])
            b = second[0, :, k].reshape(a.shape)
            parts = b.astype(jnp.float32).reshape(first.shape[1], 2, GROUP, a.shape[1])
            turned = jnp.concatenate([-parts[:, 1:], parts[:, :1]], axis=1)
            turned = turned.reshape(a.shape).astype(jnp.bfloat16)
            for e, m in enumerate((b, turned)):
                out[0, 0, 0, e, k] = lax.dot_general(
                    a, m, (((0,), (0,)), ((), ())), preferred_element_type=jnp.float32
                ).astype(jnp.bfloat16)

    @pl.when(jnp.logical_not(live))
    def _():
        out[...] = jnp.zeros_like(out)


def cross(sets, pairs, count, place, rows, owned):
    _, groups, bins, entries, channels = sets.shape
    step = math.gcd(bins, 4)
    block = (1, groups, step, entries, channels)

    def first_map(s, k, pairs, count, place):
        i = pairs[2 * (place[0] + s)]
        return jnp.where(i == place[2], place[1], rows + i), 0, k, 0, 0

    def second_map(s, k, pairs, count, place):
        return pairs[2 * (place[0] + s) + 1], 0, k, 0, 0

    return pl.pallas_call(
        cross_kernel,
        out_shape=jax.ShapeDtypeStruct(
            (1, 1, owned, 2, bins, channels, channels), jnp.bfloat16),
        grid_spec=pltpu.PrefetchScalarGridSpec(
            num_scalar_prefetch=3,
            grid=(owned, bins // step),
            in_specs=[
                pl.BlockSpec(block, first_map),
                pl.BlockSpec(block, second_map),
            ],
            out_specs=pl.BlockSpec(
                (1, 1, 1, 2, step, channels, channels), lambda s, k, *_: (0, 0, s, 0, k, 0, 0)),
        ),
        compiler_params=pltpu.CompilerParams(vmem_limit_bytes=40 * 2**20),
        cost_estimate=pl.CostEstimate(
            flops=4 * owned * bins * channels * channels * groups * entries,
            bytes_accessed=4 * owned * bins * channels * channels, transcendentals=0),
    )(pairs, count, place, sets, sets)


def body(records, tile_pairs, tile_count, bin_index):
    rows, cols = lax.axis_size("row"), lax.axis_size("col")
    r, q = lax.axis_index("row"), lax.axis_index("col")
    sets = gather(records, dft_tables(bin_index, records.shape[2]), rows, cols)
    owned = tile_pairs.shape[2] // lax.axis_size("win")
    place = jnp.stack([lax.axis_index("win") * owned, r, q]).astype(jnp.int32)
    return cross(sets, tile_pairs.reshape(-1), tile_count.reshape(-1), place, rows, owned)


def solution(mesh):
    return jax.shard_map(
        body,
        mesh=mesh,
        in_specs=(
            P("win", ("row", "col"), None),
            P("row", "col", None, None),
            P("row", "col"),
            P(),
        ),
        out_specs=P("row", "col", "win", None, None, None, None),
        check_vma=False,
    )
```

```python
import functools
import math

import jax
import jax.numpy as jnp
from jax import lax
from jax.experimental import pallas as pl
from jax.experimental.pallas import tpu as pltpu
from jax.sharding import PartitionSpec as P

GROUP = 8
UP, DOWN, PARTNER, RIGHT, LEFT, SIBLING = range(6)


def dft_tables(bin_index, length):
    sample_ids = jnp.arange(length, dtype=jnp.int32)
    phases = bin_index[:, None] * sample_ids[None, :] % length
    angles = 2.0 * math.pi / length * phases.astype(jnp.float32)
    window_taper = 0.5 - 0.5 * jnp.cos(2.0 * math.pi / length * sample_ids.astype(jnp.float32))
    cosine = window_taper[None, :] * jnp.cos(angles)
    sine = -window_taper[None, :] * jnp.sin(angles)
    return cosine.astype(jnp.bfloat16), sine.astype(jnp.bfloat16)


def gather_kernel(rows, cols, groups, rec_hbm, cos_ref, sin_ref, sets, rec, spec, own,
                  rec_sem, local_sem, send_sem, recv_sem):
    w, r, q = lax.axis_index("win"), lax.axis_index("row"), lax.axis_index("col")
    chips = cols // 2
    x = q // 2
    other = 1 - w
    sib = q + 1 - 2 * (q % 2)
    mine, theirs = w * groups, other * groups
    device = {
        UP: (w, r + 1, q), DOWN: (w, r - 1, q), PARTNER: (other, r, q),
        RIGHT: (w, r, q + 2), LEFT: (w, r, q - 2), SIBLING: (w, r, sib),
    }
    exists = {
        UP: r < rows - 1, DOWN: r > 0, PARTNER: None,
        RIGHT: x < chips - 1, LEFT: x > 0, SIBLING: None,
    }

    def fetch(i):
        part = pl.ds(i * GROUP, GROUP)
        return pltpu.make_async_copy(rec_hbm.at[part], rec.at[part], rec_sem.at[i])

    for i in range(groups):
        fetch(i).start()

    def guarded(way, f):
        if exists[way] is None:
            f()
        else:
            pl.when(exists[way])(f)

    barrier = pltpu.get_barrier_semaphore()
    for way in range(6):
        guarded(way, lambda way=way: pl.semaphore_signal(
            barrier, inc=1, device_id=device[way], device_id_type=pl.DeviceIdType.MESH))
    ends = sum(exists[way].astype(jnp.int32) for way in (UP, DOWN, RIGHT, LEFT))
    pl.semaphore_wait(barrier, 2 + ends)

    def copy(way, src, slot, g):
        return pltpu.make_async_remote_copy(
            src_ref=src, dst_ref=sets.at[slot, g], send_sem=send_sem.at[way, slot, g],
            recv_sem=recv_sem.at[slot, g], device_id=device[way],
            device_id_type=pl.DeviceIdType.MESH)

    pending = []

    def send(way, src, slot, g, cond=None):
        def go():
            guarded(way, lambda: copy(way, src, slot, g).start())

        def done():
            guarded(way, lambda: copy(way, src, slot, g).wait_send())

        if cond is None:
            go()
        pending.append((cond, done))
        return go

    def arrived(slot, g):
        copy(PARTNER, sets.at[slot, g], slot, g).wait_recv()

    bins = cos_ref.shape[0]
    keeps = []
    for i in range(groups):
        fetch(i).wait()

        def one_window(v, _, i=i):
            table = jnp.concatenate([cos_ref[...], sin_ref[...]], axis=0)
            s = lax.dot_general(table, rec[i * GROUP + v], (((1,), (1,)), ((), ())),
                                preferred_element_type=jnp.float32)
            scale = 1.0 / jnp.sqrt(jnp.mean(s * s, axis=0, keepdims=True) + 1e-06)
            s = s * scale
            for lane in range(spec.shape[0]):
                part = s[:, lane * 128:(lane + 1) * 128]
                spec[lane, pl.ds(v, bins, stride=2 * GROUP), :] = part[:bins]
                spec[lane, pl.ds(v + GROUP, bins, stride=2 * GROUP), :] = part[bins:]
            return 0

        lax.fori_loop(0, GROUP, one_window, 0)
        for lane in range(spec.shape[0]):
            own[i, :, :, lane * 128:(lane + 1) * 128] = spec[lane].astype(jnp.bfloat16).reshape(
                own.shape[1], own.shape[2], 128)
        for way in (PARTNER, UP, DOWN):
            send(way, own.at[i], r, mine + i)
        for way in (RIGHT, LEFT, SIBLING):
            send(way, own.at[i], rows + q, mine + i)
        keep = pltpu.make_async_copy(own.at[i], sets.at[r, mine + i], local_sem.at[i])
        keep.start()
        keeps.append(keep)

    def relay(cond, slot, g, ways):
        goes = [send(way, sets.at[slot, g], slot, g, cond) for way in ways]

        def go():
            arrived(slot, g)
            for f in goes:
                f()

        pl.when(cond)(go)

    def along_x(g):
        for d in range(1, chips):
            relay(x - d >= 0, rows + q - 2 * d, g, (RIGHT, SIBLING))
            relay(x + d < chips, rows + q + 2 * d, g, (LEFT, SIBLING))

    for h in range(1, rows):
        for i in range(groups):
            if h == 1:
                arrived(r, theirs + i)
                for way in (RIGHT, LEFT, SIBLING):
                    send(way, sets.at[r, theirs + i], rows + q, theirs + i)
            shared = () if h == 1 and i == groups - 1 else (PARTNER,)
            relay(r - h >= 0, r - h, mine + i, (UP,) + shared)
            relay(r + h < rows, r + h, mine + i, (DOWN,) + shared)
        if h == 1:
            for i in range(groups):
                along_x(mine + i)
    for way in (UP, DOWN):
        send(way, sets.at[r, theirs + groups - 1], r, theirs + groups - 1)
    for i in range(groups):
        along_x(theirs + i)

    for h in range(1, rows):
        for i in range(groups):
            pl.when(r - h >= 0)(lambda h=h, i=i: arrived(r - h, theirs + i))
            pl.when(r + h < rows)(lambda h=h, i=i: arrived(r + h, theirs + i))
    for c in range(chips):
        for g in range(2 * groups):
            arrived(rows + 2 * c + 1 - q % 2, g)
    for keep in keeps:
        keep.wait()
    for cond, done in pending:
        if cond is None:
            done()
        else:
            pl.when(cond)(done)


def gather(records, tables, rows, cols):
    windows, channels, length = records.shape
    groups = windows // GROUP
    entries = 2 * tables[0].shape[0]
    bins = entries // 2
    slots = rows + cols
    return pl.pallas_call(
        functools.partial(gather_kernel, rows, cols, groups),
        out_shape=jax.ShapeDtypeStruct(
            (slots, 2 * groups, bins, 2 * GROUP, channels), jnp.bfloat16),
        in_specs=[pl.BlockSpec(memory_space=pl.ANY)] + [pl.BlockSpec(memory_space=pltpu.VMEM)] * 2,
        out_specs=pl.BlockSpec(memory_space=pl.ANY),
        scratch_shapes=[
            pltpu.VMEM(records.shape, jnp.bfloat16),
            pltpu.VMEM((channels // 128, entries * GROUP, 128), jnp.float32),
            pltpu.VMEM((groups, bins, 2 * GROUP, channels), jnp.bfloat16),
            pltpu.SemaphoreType.DMA((groups,)),
            pltpu.SemaphoreType.DMA((groups,)),
            pltpu.SemaphoreType.DMA((6, slots, 2 * groups)),
            pltpu.SemaphoreType.DMA((slots, 2 * groups)),
        ],
        compiler_params=pltpu.CompilerParams(
            collective_id=0, has_side_effects=True, vmem_limit_bytes=40 * 2**20),
        cost_estimate=pl.CostEstimate(
            flops=2 * windows * channels * length * entries,
            bytes_accessed=windows * channels * length * 2, transcendentals=0),
    )(records, *tables)


def cross_kernel(rows, owned, pairs, count, place, sets, out, ring, sem):
    depth, _, step, channels, _ = ring.shape
    groups = sets.shape[1]
    chunks = out.shape[4] // step

    def copy(n):
        part = pl.ds((n % chunks) * step, step)
        return pltpu.make_async_copy(
            ring.at[n % depth], out.at[0, 0, n // chunks, :, part], sem.at[n % depth])

    def one(n, _):
        slot = n % depth
        position = place[0] + n // chunks
        i, j = pairs[2 * position], pairs[2 * position + 1]
        first = jnp.where(i == place[2], place[1], rows + i)
        live = position < count[0]

        @pl.when(n >= depth)
        def _():
            copy(n - depth).wait()

        @pl.when(live)
        def _():
            for t in range(step):
                k = (n % chunks) * step + t
                a = sets[first, :, k].reshape(-1, channels)
                b = sets[j, :, k].reshape(a.shape)
                parts = b.astype(jnp.float32).reshape(groups, 2, GROUP, channels)
                turned = jnp.concatenate([-parts[:, 1:], parts[:, :1]], axis=1)
                turned = turned.reshape(a.shape).astype(jnp.bfloat16)
                both = lax.dot_general(
                    a, jnp.concatenate([b, turned], axis=1), (((0,), (0,)), ((), ())),
                    preferred_element_type=jnp.float32)
                ring[slot, 0, t] = both[:, :channels].astype(jnp.bfloat16)
                ring[slot, 1, t] = both[:, channels:].astype(jnp.bfloat16)

        @pl.when(jnp.logical_not(live))
        def _():
            ring[slot] = jnp.zeros(ring.shape[1:], jnp.bfloat16)

        copy(n).start()
        return 0

    total = owned * chunks
    lax.fori_loop(0, total, one, 0)
    for n in range(max(total - depth, 0), total):
        copy(n).wait()


def cross(sets, pairs, count, place, rows, owned):
    _, groups, bins, entries, channels = sets.shape
    step = math.gcd(bins, 4)
    smem = pl.BlockSpec(memory_space=pltpu.SMEM)
    return pl.pallas_call(
        functools.partial(cross_kernel, rows, owned),
        out_shape=jax.ShapeDtypeStruct(
            (1, 1, owned, 2, bins, channels, channels), jnp.bfloat16),
        in_specs=[smem, smem, smem, pl.BlockSpec(memory_space=pltpu.VMEM)],
        out_specs=pl.BlockSpec(memory_space=pl.ANY),
        scratch_shapes=[
            pltpu.VMEM((4, 2, step, channels, channels), jnp.bfloat16),
            pltpu.SemaphoreType.DMA((4,)),
        ],
        compiler_params=pltpu.CompilerParams(vmem_limit_bytes=40 * 2**20),
        cost_estimate=pl.CostEstimate(
            flops=4 * owned * bins * channels * channels * groups * entries,
            bytes_accessed=4 * owned * bins * channels * channels, transcendentals=0),
    )(pairs, count, place, sets)


def body(records, tile_pairs, tile_count, bin_index):
    rows, cols = lax.axis_size("row"), lax.axis_size("col")
    r, q = lax.axis_index("row"), lax.axis_index("col")
    sets = gather(records, dft_tables(bin_index, records.shape[2]), rows, cols)
    owned = tile_pairs.shape[2] // lax.axis_size("win")
    place = jnp.stack([lax.axis_index("win") * owned, r, q]).astype(jnp.int32)
    return cross(sets, tile_pairs.reshape(-1), tile_count.reshape(-1), place, rows, owned)


def solution(mesh):
    return jax.shard_map(
        body,
        mesh=mesh,
        in_specs=(
            P("win", ("row", "col"), None),
            P("row", "col", None, None),
            P("row", "col"),
            P(),
        ),
        out_specs=P("row", "col", "win", None, None, None, None),
        check_vma=False,
    )
```

```python
import functools
import math

import jax
import jax.numpy as jnp
from jax import lax
from jax.experimental import pallas as pl
from jax.experimental.pallas import tpu as pltpu
from jax.sharding import PartitionSpec as P

GROUP = 8
UP, DOWN, PARTNER, RIGHT, LEFT, SIBLING = range(6)


def dft_tables(bin_index, length):
    sample_ids = jnp.arange(length, dtype=jnp.int32)
    phases = bin_index[:, None] * sample_ids[None, :] % length
    angles = 2.0 * math.pi / length * phases.astype(jnp.float32)
    window_taper = 0.5 - 0.5 * jnp.cos(2.0 * math.pi / length * sample_ids.astype(jnp.float32))
    cosine = window_taper[None, :] * jnp.cos(angles)
    sine = -window_taper[None, :] * jnp.sin(angles)
    return cosine.astype(jnp.bfloat16), sine.astype(jnp.bfloat16)


def gather_kernel(rows, cols, groups, rec_hbm, cos_ref, sin_ref, sets, rec, spec, own,
                  rec_sem, local_sem, send_sem, recv_sem):
    w, r, q = lax.axis_index("win"), lax.axis_index("row"), lax.axis_index("col")
    chips = cols // 2
    x = q // 2
    other = 1 - w
    sib = q + 1 - 2 * (q % 2)
    mine, theirs = w * groups, other * groups
    device = {
        UP: (w, r + 1, q), DOWN: (w, r - 1, q), PARTNER: (other, r, q),
        RIGHT: (w, r, q + 2), LEFT: (w, r, q - 2), SIBLING: (w, r, sib),
    }
    exists = {
        UP: r < rows - 1, DOWN: r > 0, PARTNER: None,
        RIGHT: x < chips - 1, LEFT: x > 0, SIBLING: None,
    }

    def fetch(i):
        part = pl.ds(i * GROUP, GROUP)
        return pltpu.make_async_copy(rec_hbm.at[part], rec.at[part], rec_sem.at[i])

    for i in range(groups):
        fetch(i).start()

    def guarded(way, f):
        if exists[way] is None:
            f()
        else:
            pl.when(exists[way])(f)

    barrier = pltpu.get_barrier_semaphore()
    for way in range(6):
        guarded(way, lambda way=way: pl.semaphore_signal(
            barrier, inc=1, device_id=device[way], device_id_type=pl.DeviceIdType.MESH))
    ends = sum(exists[way].astype(jnp.int32) for way in (UP, DOWN, RIGHT, LEFT))
    pl.semaphore_wait(barrier, 2 + ends)

    def copy(way, src, slot, g):
        return pltpu.make_async_remote_copy(
            src_ref=src, dst_ref=sets.at[slot, g], send_sem=send_sem.at[way, slot, g],
            recv_sem=recv_sem.at[slot, g], device_id=device[way],
            device_id_type=pl.DeviceIdType.MESH)

    pending = []

    def send(way, src, slot, g, cond=None):
        def go():
            guarded(way, lambda: copy(way, src, slot, g).start())

        def done():
            guarded(way, lambda: copy(way, src, slot, g).wait_send())

        if cond is None:
            go()
        pending.append((cond, done))
        return go

    def arrived(slot, g):
        copy(PARTNER, sets.at[slot, g], slot, g).wait_recv()

    bins = cos_ref.shape[0]
    keeps = []
    for i in range(groups):
        fetch(i).wait()

        def one_window(v, _, i=i):
            table = jnp.concatenate([cos_ref[...], sin_ref[...]], axis=0)
            s = lax.dot_general(table, rec[i * GROUP + v], (((1,), (1,)), ((), ())),
                                preferred_element_type=jnp.float32)
            scale = 1.0 / jnp.sqrt(jnp.mean(s * s, axis=0, keepdims=True) + 1e-06)
            s = s * scale
            for lane in range(spec.shape[0]):
                part = s[:, lane * 128:(lane + 1) * 128]
                spec[lane, pl.ds(v, bins, stride=2 * GROUP), :] = part[:bins]
                spec[lane, pl.ds(v + GROUP, bins, stride=2 * GROUP), :] = part[bins:]
            return 0

        lax.fori_loop(0, GROUP, one_window, 0, unroll=4)
        for lane in range(spec.shape[0]):
            own[i, :, :, lane * 128:(lane + 1) * 128] = spec[lane].astype(jnp.bfloat16).reshape(
                own.shape[1], own.shape[2], 128)
        for way in (PARTNER, UP, DOWN):
            send(way, own.at[i], r, mine + i)
        for way in (RIGHT, LEFT, SIBLING):
            send(way, own.at[i], rows + q, mine + i)
        keep = pltpu.make_async_copy(own.at[i], sets.at[r, mine + i], local_sem.at[i])
        keep.start()
        keeps.append(keep)

    def relay(cond, slot, g, ways):
        goes = [send(way, sets.at[slot, g], slot, g, cond) for way in ways]

        def go():
            arrived(slot, g)
            for f in goes:
                f()

        pl.when(cond)(go)

    def along_x(g):
        for d in range(1, chips):
            relay(x - d >= 0, rows + q - 2 * d, g, (RIGHT, SIBLING))
            relay(x + d < chips, rows + q + 2 * d, g, (LEFT, SIBLING))

    def extra(up, down):
        g = theirs + groups - 1
        for way, cond in ((UP, up), (DOWN, down)):
            pl.when(cond)(send(way, sets.at[r, g], r, g, cond))

    for h in range(1, rows):
        for i in range(groups):
            if h == 1:
                arrived(r, theirs + i)
                for way in (RIGHT, LEFT, SIBLING):
                    send(way, sets.at[r, theirs + i], rows + q, theirs + i)
            if h == 1 and i == groups - 1:
                extra(r < rows - 2, r > 1)
            shared = () if h == 1 and i == groups - 1 else (PARTNER,)
            relay(r - h >= 0, r - h, mine + i, (UP,) + shared)
            relay(r + h < rows, r + h, mine + i, (DOWN,) + shared)
        if h == 1:
            for i in range(groups):
                along_x(mine + i)
        if h == max(1, rows - 2):
            for i in range(groups):
                along_x(theirs + i)
    extra(r == rows - 2, r == 1)

    for h in range(1, rows):
        for i in range(groups):
            pl.when(r - h >= 0)(lambda h=h, i=i: arrived(r - h, theirs + i))
            pl.when(r + h < rows)(lambda h=h, i=i: arrived(r + h, theirs + i))
    for c in range(chips):
        for g in range(2 * groups):
            arrived(rows + 2 * c + 1 - q % 2, g)
    for keep in keeps:
        keep.wait()
    for cond, done in pending:
        if cond is None:
            done()
        else:
            pl.when(cond)(done)


def gather(records, tables, rows, cols):
    windows, channels, length = records.shape
    groups = windows // GROUP
    entries = 2 * tables[0].shape[0]
    bins = entries // 2
    slots = rows + cols
    return pl.pallas_call(
        functools.partial(gather_kernel, rows, cols, groups),
        out_shape=jax.ShapeDtypeStruct(
            (slots, 2 * groups, bins, 2 * GROUP, channels), jnp.bfloat16),
        in_specs=[pl.BlockSpec(memory_space=pl.ANY)] + [pl.BlockSpec(memory_space=pltpu.VMEM)] * 2,
        out_specs=pl.BlockSpec(memory_space=pl.ANY),
        scratch_shapes=[
            pltpu.VMEM(records.shape, jnp.bfloat16),
            pltpu.VMEM((channels // 128, entries * GROUP, 128), jnp.float32),
            pltpu.VMEM((groups, bins, 2 * GROUP, channels), jnp.bfloat16),
            pltpu.SemaphoreType.DMA((groups,)),
            pltpu.SemaphoreType.DMA((groups,)),
            pltpu.SemaphoreType.DMA((6, slots, 2 * groups)),
            pltpu.SemaphoreType.DMA((slots, 2 * groups)),
        ],
        compiler_params=pltpu.CompilerParams(
            collective_id=0, has_side_effects=True, vmem_limit_bytes=40 * 2**20),
        cost_estimate=pl.CostEstimate(
            flops=2 * windows * channels * length * entries,
            bytes_accessed=windows * channels * length * 2, transcendentals=0),
    )(records, *tables)


def cross_kernel(rows, owned, pairs, count, place, sets, out, ring, sem):
    depth, _, step, channels, _ = ring.shape
    groups = sets.shape[1]
    chunks = out.shape[4] // step

    def copy(n):
        part = pl.ds((n % chunks) * step, step)
        return pltpu.make_async_copy(
            ring.at[n % depth], out.at[0, 0, n // chunks, :, part], sem.at[n % depth])

    def one(n, _):
        slot = n % depth
        position = place[0] + n // chunks
        i, j = pairs[0, 0, 0, position], pairs[0, 0, 1, position]
        first = jnp.where(i == place[2], place[1], rows + i)
        live = position < count[0]

        @pl.when(n >= depth)
        def _():
            copy(n - depth).wait()

        @pl.when(live)
        def _():
            for t in range(step):
                k = (n % chunks) * step + t
                a = sets[first, :, k].reshape(-1, channels)
                b = sets[j, :, k].reshape(a.shape)
                parts = b.astype(jnp.float32).reshape(groups, 2, GROUP, channels)
                turned = jnp.concatenate([-parts[:, 1:], parts[:, :1]], axis=1)
                turned = turned.reshape(a.shape).astype(jnp.bfloat16)
                both = lax.dot_general(
                    a, jnp.concatenate([b, turned], axis=1), (((0,), (0,)), ((), ())),
                    preferred_element_type=jnp.float32)
                ring[slot, 0, t] = both[:, :channels].astype(jnp.bfloat16)
                ring[slot, 1, t] = both[:, channels:].astype(jnp.bfloat16)

        @pl.when(jnp.logical_not(live))
        def _():
            ring[slot] = jnp.zeros(ring.shape[1:], jnp.bfloat16)

        copy(n).start()
        return 0

    total = owned * chunks
    lax.fori_loop(0, total, one, 0)
    for n in range(max(total - depth, 0), total):
        copy(n).wait()


def cross(sets, pairs, count, place, rows, owned):
    _, groups, bins, entries, channels = sets.shape
    step = math.gcd(bins, 4)
    smem = pl.BlockSpec(memory_space=pltpu.SMEM)
    return pl.pallas_call(
        functools.partial(cross_kernel, rows, owned),
        out_shape=jax.ShapeDtypeStruct(
            (1, 1, owned, 2, bins, channels, channels), jnp.bfloat16),
        in_specs=[smem, smem, smem, pl.BlockSpec(memory_space=pltpu.VMEM)],
        out_specs=pl.BlockSpec(memory_space=pl.ANY),
        scratch_shapes=[
            pltpu.VMEM((4, 2, step, channels, channels), jnp.bfloat16),
            pltpu.SemaphoreType.DMA((4,)),
        ],
        compiler_params=pltpu.CompilerParams(vmem_limit_bytes=40 * 2**20),
        cost_estimate=pl.CostEstimate(
            flops=4 * owned * bins * channels * channels * groups * entries,
            bytes_accessed=4 * owned * bins * channels * channels, transcendentals=0),
    )(pairs, count, place, sets)


def body(records, tile_pairs, tile_count, bin_index):
    rows, cols = lax.axis_size("row"), lax.axis_size("col")
    r, q = lax.axis_index("row"), lax.axis_index("col")
    sets = gather(records, dft_tables(bin_index, records.shape[2]), rows, cols)
    owned = tile_pairs.shape[2] // lax.axis_size("win")
    place = jnp.stack([lax.axis_index("win") * owned, r, q]).astype(jnp.int32)
    return cross(sets, jnp.swapaxes(tile_pairs, 2, 3), tile_count.reshape(-1), place, rows, owned)


def solution(mesh):
    return jax.shard_map(
        body,
        mesh=mesh,
        in_specs=(
            P("win", ("row", "col"), None),
            P("row", "col", None, None),
            P("row", "col"),
            P(),
        ),
        out_specs=P("row", "col", "win", None, None, None, None),
        check_vma=False,
    )
```

```python
import functools
import math

import jax
import jax.numpy as jnp
from jax import lax
from jax.experimental import pallas as pl
from jax.experimental.pallas import tpu as pltpu
from jax.sharding import PartitionSpec as P

GROUP = 8
UP, DOWN, PARTNER, RIGHT, LEFT, SIBLING = range(6)


def dft_tables(bin_index, length):
    sample_ids = jnp.arange(length, dtype=jnp.int32)
    phases = bin_index[:, None] * sample_ids[None, :] % length
    angles = 2.0 * math.pi / length * phases.astype(jnp.float32)
    window_taper = 0.5 - 0.5 * jnp.cos(2.0 * math.pi / length * sample_ids.astype(jnp.float32))
    cosine = window_taper[None, :] * jnp.cos(angles)
    sine = -window_taper[None, :] * jnp.sin(angles)
    return cosine.astype(jnp.bfloat16), sine.astype(jnp.bfloat16)


def gather_kernel(rows, cols, groups, rec_hbm, cos_ref, sin_ref, sets, rec, spec, own,
                  rec_sem, local_sem, send_sem, recv_sem):
    w, r, q = lax.axis_index("win"), lax.axis_index("row"), lax.axis_index("col")
    chips = cols // 2
    x = q // 2
    other = 1 - w
    sib = q + 1 - 2 * (q % 2)
    mine, theirs = w * groups, other * groups
    device = {
        UP: (w, r + 1, q), DOWN: (w, r - 1, q), PARTNER: (other, r, q),
        RIGHT: (w, r, q + 2), LEFT: (w, r, q - 2), SIBLING: (w, r, sib),
    }
    exists = {
        UP: r < rows - 1, DOWN: r > 0, PARTNER: None,
        RIGHT: x < chips - 1, LEFT: x > 0, SIBLING: None,
    }

    def fetch(i):
        part = pl.ds(i * GROUP, GROUP)
        return pltpu.make_async_copy(rec_hbm.at[part], rec.at[part], rec_sem.at[i])

    for i in range(groups):
        fetch(i).start()

    def guarded(way, f):
        if exists[way] is None:
            f()
        else:
            pl.when(exists[way])(f)

    barrier = pltpu.get_barrier_semaphore()
    for way in range(6):
        guarded(way, lambda way=way: pl.semaphore_signal(
            barrier, inc=1, device_id=device[way], device_id_type=pl.DeviceIdType.MESH))
    ends = sum(exists[way].astype(jnp.int32) for way in (UP, DOWN, RIGHT, LEFT))

    def copy(way, src, slot, g):
        return pltpu.make_async_remote_copy(
            src_ref=src, dst_ref=sets.at[slot, g], send_sem=send_sem.at[way, slot, g],
            recv_sem=recv_sem.at[slot, g], device_id=device[way],
            device_id_type=pl.DeviceIdType.MESH)

    pending = []

    def send(way, src, slot, g, cond=None):
        def go():
            guarded(way, lambda: copy(way, src, slot, g).start())

        def done():
            guarded(way, lambda: copy(way, src, slot, g).wait_send())

        if cond is None:
            go()
        pending.append((cond, done))
        return go

    def arrived(slot, g):
        copy(PARTNER, sets.at[slot, g], slot, g).wait_recv()

    bins = cos_ref.shape[0]
    keeps = []
    for i in range(groups):
        fetch(i).wait()

        def one_window(v, _, i=i):
            table = jnp.concatenate([cos_ref[...], sin_ref[...]], axis=0)
            s = lax.dot_general(table, rec[i * GROUP + v], (((1,), (1,)), ((), ())),
                                preferred_element_type=jnp.float32)
            scale = 1.0 / jnp.sqrt(jnp.mean(s * s, axis=0, keepdims=True) + 1e-06)
            s = s * scale
            for lane in range(spec.shape[0]):
                part = s[:, lane * 128:(lane + 1) * 128]
                spec[lane, pl.ds(v, bins, stride=2 * GROUP), :] = part[:bins]
                spec[lane, pl.ds(v + GROUP, bins, stride=2 * GROUP), :] = part[bins:]
            return 0

        lax.fori_loop(0, GROUP, one_window, 0, unroll=4)
        for lane in range(spec.shape[0]):
            own[i, :, :, lane * 128:(lane + 1) * 128] = spec[lane].astype(jnp.bfloat16).reshape(
                own.shape[1], own.shape[2], 128)
        if i == 0:
            pl.semaphore_wait(barrier, 2 + ends)
        for way in (PARTNER, UP, DOWN):
            send(way, own.at[i], r, mine + i)
        for way in (RIGHT, LEFT, SIBLING):
            send(way, own.at[i], rows + q, mine + i)
        keep = pltpu.make_async_copy(own.at[i], sets.at[r, mine + i], local_sem.at[i])
        keep.start()
        keeps.append(keep)

    def relay(cond, slot, g, ways):
        goes = [send(way, sets.at[slot, g], slot, g, cond) for way in ways]

        def go():
            arrived(slot, g)
            for f in goes:
                f()

        pl.when(cond)(go)

    def along_x(g):
        for d in range(1, chips):
            relay(x - d >= 0, rows + q - 2 * d, g, (RIGHT, SIBLING))
            relay(x + d < chips, rows + q + 2 * d, g, (LEFT, SIBLING))

    def extra(up, down):
        g = theirs + groups - 1
        for way, cond in ((UP, up), (DOWN, down)):
            pl.when(cond)(send(way, sets.at[r, g], r, g, cond))

    for h in range(1, rows):
        for i in range(groups):
            if h == 1:
                arrived(r, theirs + i)
                for way in (RIGHT, LEFT, SIBLING):
                    send(way, sets.at[r, theirs + i], rows + q, theirs + i)
            if h == 1 and i == groups - 1:
                extra(r < rows - 2, r > 1)
            shared = () if h == 1 and i == groups - 1 else (PARTNER,)
            relay(r - h >= 0, r - h, mine + i, (UP,) + shared)
            relay(r + h < rows, r + h, mine + i, (DOWN,) + shared)
        if h == 1:
            for i in range(groups):
                along_x(mine + i)
        if h == max(1, rows - 2):
            for i in range(groups):
                along_x(theirs + i)
    extra(r == rows - 2, r == 1)

    for h in range(1, rows):
        for i in range(groups):
            pl.when(r - h >= 0)(lambda h=h, i=i: arrived(r - h, theirs + i))
            pl.when(r + h < rows)(lambda h=h, i=i: arrived(r + h, theirs + i))
    for c in range(chips):
        for g in range(2 * groups):
            arrived(rows + 2 * c + 1 - q % 2, g)
    for keep in keeps:
        keep.wait()
    for cond, done in pending:
        if cond is None:
            done()
        else:
            pl.when(cond)(done)


def gather(records, tables, rows, cols):
    windows, channels, length = records.shape
    groups = windows // GROUP
    entries = 2 * tables[0].shape[0]
    bins = entries // 2
    slots = rows + cols
    return pl.pallas_call(
        functools.partial(gather_kernel, rows, cols, groups),
        out_shape=jax.ShapeDtypeStruct(
            (slots, 2 * groups, bins, 2 * GROUP, channels), jnp.bfloat16),
        in_specs=[pl.BlockSpec(memory_space=pl.ANY)] + [pl.BlockSpec(memory_space=pltpu.VMEM)] * 2,
        out_specs=pl.BlockSpec(memory_space=pl.ANY),
        scratch_shapes=[
            pltpu.VMEM(records.shape, jnp.bfloat16),
            pltpu.VMEM((channels // 128, entries * GROUP, 128), jnp.float32),
            pltpu.VMEM((groups, bins, 2 * GROUP, channels), jnp.bfloat16),
            pltpu.SemaphoreType.DMA((groups,)),
            pltpu.SemaphoreType.DMA((groups,)),
            pltpu.SemaphoreType.DMA((6, slots, 2 * groups)),
            pltpu.SemaphoreType.DMA((slots, 2 * groups)),
        ],
        compiler_params=pltpu.CompilerParams(
            collective_id=0, has_side_effects=True, vmem_limit_bytes=40 * 2**20),
        cost_estimate=pl.CostEstimate(
            flops=2 * windows * channels * length * entries,
            bytes_accessed=windows * channels * length * 2, transcendentals=0),
    )(records, *tables)


def cross_kernel(rows, owned, pairs, count, place, sets, out, ring, sem):
    depth, _, step, channels, _ = ring.shape
    groups = sets.shape[1]
    chunks = out.shape[4] // step

    def copy(n):
        part = pl.ds((n % chunks) * step, step)
        return pltpu.make_async_copy(
            ring.at[n % depth], out.at[0, 0, n // chunks, :, part], sem.at[n % depth])

    def one(n, _):
        slot = n % depth
        position = place[0] + n // chunks
        i, j = pairs[0, 0, 0, position], pairs[0, 0, 1, position]
        first = jnp.where(i == place[2], place[1], rows + i)
        live = position < count[0]

        @pl.when(n >= depth)
        def _():
            copy(n - depth).wait()

        @pl.when(live)
        def _():
            for t in range(step):
                k = (n % chunks) * step + t
                a = sets[first, :, k].reshape(-1, channels)
                b = sets[j, :, k].reshape(a.shape)
                parts = b.astype(jnp.float32).reshape(groups, 2, GROUP, channels)
                turned = jnp.concatenate([-parts[:, 1:], parts[:, :1]], axis=1)
                turned = turned.reshape(a.shape).astype(jnp.bfloat16)
                both = lax.dot_general(
                    a, jnp.concatenate([b, turned], axis=1), (((0,), (0,)), ((), ())),
                    preferred_element_type=jnp.float32)
                ring[slot, 0, t] = both[:, :channels].astype(jnp.bfloat16)
                ring[slot, 1, t] = both[:, channels:].astype(jnp.bfloat16)

        @pl.when(jnp.logical_not(live))
        def _():
            ring[slot] = jnp.zeros(ring.shape[1:], jnp.bfloat16)

        copy(n).start()
        return 0

    total = owned * chunks
    lax.fori_loop(0, total, one, 0)
    for n in range(max(total - depth, 0), total):
        copy(n).wait()


def cross(sets, pairs, count, place, rows, owned):
    _, groups, bins, entries, channels = sets.shape
    step = math.gcd(bins, 8)
    smem = pl.BlockSpec(memory_space=pltpu.SMEM)
    return pl.pallas_call(
        functools.partial(cross_kernel, rows, owned),
        out_shape=jax.ShapeDtypeStruct(
            (1, 1, owned, 2, bins, channels, channels), jnp.bfloat16),
        in_specs=[smem, smem, smem, pl.BlockSpec(memory_space=pltpu.VMEM)],
        out_specs=pl.BlockSpec(memory_space=pl.ANY),
        scratch_shapes=[
            pltpu.VMEM((4, 2, step, channels, channels), jnp.bfloat16),
            pltpu.SemaphoreType.DMA((4,)),
        ],
        compiler_params=pltpu.CompilerParams(vmem_limit_bytes=40 * 2**20),
        cost_estimate=pl.CostEstimate(
            flops=4 * owned * bins * channels * channels * groups * entries,
            bytes_accessed=4 * owned * bins * channels * channels, transcendentals=0),
    )(pairs, count, place, sets)


def body(records, tile_pairs, tile_count, bin_index):
    rows, cols = lax.axis_size("row"), lax.axis_size("col")
    r, q = lax.axis_index("row"), lax.axis_index("col")
    sets = gather(records, dft_tables(bin_index, records.shape[2]), rows, cols)
    owned = tile_pairs.shape[2] // lax.axis_size("win")
    place = jnp.stack([lax.axis_index("win") * owned, r, q]).astype(jnp.int32)
    return cross(sets, jnp.swapaxes(tile_pairs, 2, 3), tile_count.reshape(-1), place, rows, owned)


def solution(mesh):
    return jax.shard_map(
        body,
        mesh=mesh,
        in_specs=(
            P("win", ("row", "col"), None),
            P("row", "col", None, None),
            P("row", "col"),
            P(),
        ),
        out_specs=P("row", "col", "win", None, None, None, None),
        check_vma=False,
    )
```

```python
import functools
import math

import jax
import jax.numpy as jnp
from jax import lax
from jax.experimental import pallas as pl
from jax.experimental.pallas import tpu as pltpu
from jax.sharding import PartitionSpec as P

GROUP = 8
UP, DOWN, PARTNER, RIGHT, LEFT, SIBLING = range(6)


def dft_tables(bin_index, length):
    sample_ids = jnp.arange(length, dtype=jnp.int32)
    phases = bin_index[:, None] * sample_ids[None, :] % length
    angles = 2.0 * math.pi / length * phases.astype(jnp.float32)
    window_taper = 0.5 - 0.5 * jnp.cos(2.0 * math.pi / length * sample_ids.astype(jnp.float32))
    cosine = window_taper[None, :] * jnp.cos(angles)
    sine = -window_taper[None, :] * jnp.sin(angles)
    return cosine.astype(jnp.bfloat16), sine.astype(jnp.bfloat16)


def gather_kernel(rows, cols, groups, rec_hbm, cos_ref, sin_ref, sets, rec, spec, own,
                  rec_sem, local_sem, send_sem, recv_sem):
    w, r, q = lax.axis_index("win"), lax.axis_index("row"), lax.axis_index("col")
    chips = cols // 2
    x = q // 2
    other = 1 - w
    sib = q + 1 - 2 * (q % 2)
    mine, theirs = w * groups, other * groups
    device = {
        UP: (w, r + 1, q), DOWN: (w, r - 1, q), PARTNER: (other, r, q),
        RIGHT: (w, r, q + 2), LEFT: (w, r, q - 2), SIBLING: (w, r, sib),
    }
    exists = {
        UP: r < rows - 1, DOWN: r > 0, PARTNER: None,
        RIGHT: x < chips - 1, LEFT: x > 0, SIBLING: None,
    }

    def fetch(i):
        part = pl.ds(i * GROUP, GROUP)
        return pltpu.make_async_copy(rec_hbm.at[part], rec.at[part], rec_sem.at[i])

    for i in range(groups):
        fetch(i).start()

    def guarded(way, f):
        if exists[way] is None:
            f()
        else:
            pl.when(exists[way])(f)

    barrier = pltpu.get_barrier_semaphore()
    for way in range(6):
        guarded(way, lambda way=way: pl.semaphore_signal(
            barrier, inc=1, device_id=device[way], device_id_type=pl.DeviceIdType.MESH))
    ends = sum(exists[way].astype(jnp.int32) for way in (UP, DOWN, RIGHT, LEFT))

    def copy(way, src, slot, g):
        return pltpu.make_async_remote_copy(
            src_ref=src, dst_ref=sets.at[slot, g], send_sem=send_sem.at[way, slot, g],
            recv_sem=recv_sem.at[slot, g], device_id=device[way],
            device_id_type=pl.DeviceIdType.MESH)

    pending = []

    def send(way, src, slot, g, cond=None):
        def go():
            guarded(way, lambda: copy(way, src, slot, g).start())

        def done():
            guarded(way, lambda: copy(way, src, slot, g).wait_send())

        if cond is None:
            go()
        pending.append((cond, done))
        return go

    def arrived(slot, g):
        copy(PARTNER, sets.at[slot, g], slot, g).wait_recv()

    bins = cos_ref.shape[0]
    keeps = []
    for i in range(groups):
        fetch(i).wait()

        def one_window(v, _, i=i):
            table = jnp.concatenate([cos_ref[...], sin_ref[...]], axis=0)
            s = lax.dot_general(table, rec[i * GROUP + v], (((1,), (1,)), ((), ())),
                                preferred_element_type=jnp.float32)
            scale = 1.0 / jnp.sqrt(jnp.mean(s * s, axis=0, keepdims=True) + 1e-06)
            s = s * scale
            for lane in range(spec.shape[0]):
                part = s[:, lane * 128:(lane + 1) * 128]
                spec[lane, pl.ds(v, bins, stride=2 * GROUP), :] = part[:bins]
                spec[lane, pl.ds(v + GROUP, bins, stride=2 * GROUP), :] = part[bins:]
            return 0

        lax.fori_loop(0, GROUP, one_window, 0, unroll=4)
        for lane in range(spec.shape[0]):
            own[i, :, :, lane * 128:(lane + 1) * 128] = spec[lane].astype(jnp.bfloat16).reshape(
                own.shape[1], own.shape[2], 128)
        if i == 0:
            pl.semaphore_wait(barrier, 2 + ends)
        for way in (PARTNER, UP, DOWN):
            send(way, own.at[i], r, mine + i)
        for way in (RIGHT, LEFT, SIBLING):
            send(way, own.at[i], rows + q, mine + i)
        keep = pltpu.make_async_copy(own.at[i], sets.at[r, mine + i], local_sem.at[i])
        keep.start()
        keeps.append(keep)

    def relay(cond, slot, g, ways):
        goes = [send(way, sets.at[slot, g], slot, g, cond) for way in ways]

        def go():
            arrived(slot, g)
            for f in goes:
                f()

        pl.when(cond)(go)

    def along_x(g):
        for d in range(1, chips):
            relay(x - d >= 0, rows + q - 2 * d, g, (RIGHT, SIBLING))
            relay(x + d < chips, rows + q + 2 * d, g, (LEFT, SIBLING))

    def extra(up, down):
        g = theirs + groups - 1
        for way, cond in ((UP, up), (DOWN, down)):
            pl.when(cond)(send(way, sets.at[r, g], r, g, cond))

    for h in range(1, rows):
        for i in range(groups):
            if h == 1:
                arrived(r, theirs + i)
                for way in (RIGHT, LEFT, SIBLING):
                    send(way, sets.at[r, theirs + i], rows + q, theirs + i)
            if h == 1 and i == groups - 1:
                extra(r < rows - 2, r > 1)
            shared = () if h == 1 and i == groups - 1 else (PARTNER,)
            relay(r - h >= 0, r - h, mine + i, (UP,) + shared)
            relay(r + h < rows, r + h, mine + i, (DOWN,) + shared)
        if h == 1:
            for i in range(groups):
                along_x(mine + i)
    for i in range(groups):
        along_x(theirs + i)
    extra(r == rows - 2, r == 1)

    for h in range(1, rows):
        for i in range(groups):
            pl.when(r - h >= 0)(lambda h=h, i=i: arrived(r - h, theirs + i))
            pl.when(r + h < rows)(lambda h=h, i=i: arrived(r + h, theirs + i))
    for c in range(chips):
        for g in range(2 * groups):
            arrived(rows + 2 * c + 1 - q % 2, g)
    for keep in keeps:
        keep.wait()
    for cond, done in pending:
        if cond is None:
            done()
        else:
            pl.when(cond)(done)


def gather(records, tables, rows, cols):
    windows, channels, length = records.shape
    groups = windows // GROUP
    entries = 2 * tables[0].shape[0]
    bins = entries // 2
    slots = rows + cols
    return pl.pallas_call(
        functools.partial(gather_kernel, rows, cols, groups),
        out_shape=jax.ShapeDtypeStruct(
            (slots, 2 * groups, bins, 2 * GROUP, channels), jnp.bfloat16),
        in_specs=[pl.BlockSpec(memory_space=pl.ANY)] + [pl.BlockSpec(memory_space=pltpu.VMEM)] * 2,
        out_specs=pl.BlockSpec(memory_space=pl.ANY),
        scratch_shapes=[
            pltpu.VMEM(records.shape, jnp.bfloat16),
            pltpu.VMEM((channels // 128, entries * GROUP, 128), jnp.float32),
            pltpu.VMEM((groups, bins, 2 * GROUP, channels), jnp.bfloat16),
            pltpu.SemaphoreType.DMA((groups,)),
            pltpu.SemaphoreType.DMA((groups,)),
            pltpu.SemaphoreType.DMA((6, slots, 2 * groups)),
            pltpu.SemaphoreType.DMA((slots, 2 * groups)),
        ],
        compiler_params=pltpu.CompilerParams(
            collective_id=0, has_side_effects=True, vmem_limit_bytes=40 * 2**20),
        cost_estimate=pl.CostEstimate(
            flops=2 * windows * channels * length * entries,
            bytes_accessed=windows * channels * length * 2, transcendentals=0),
    )(records, *tables)


def cross_kernel(rows, owned, pairs, count, place, sets, out, ring, sem):
    depth, _, step, channels, _ = ring.shape
    groups = sets.shape[1]
    chunks = out.shape[4] // step

    def copy(n):
        part = pl.ds((n % chunks) * step, step)
        return pltpu.make_async_copy(
            ring.at[n % depth], out.at[0, 0, n // chunks, :, part], sem.at[n % depth])

    def one(n, _):
        slot = n % depth
        position = place[0] + n // chunks
        i, j = pairs[0, 0, 0, position], pairs[0, 0, 1, position]
        first = jnp.where(i == place[2], place[1], rows + i)
        live = position < count[0]

        @pl.when(n >= depth)
        def _():
            copy(n - depth).wait()

        @pl.when(live)
        def _():
            for t in range(step):
                k = (n % chunks) * step + t
                a = sets[first, :, k].reshape(-1, channels)
                b = sets[j, :, k].reshape(a.shape)
                parts = b.astype(jnp.float32).reshape(groups, 2, GROUP, channels)
                turned = jnp.concatenate([-parts[:, 1:], parts[:, :1]], axis=1)
                turned = turned.reshape(a.shape).astype(jnp.bfloat16)
                both = lax.dot_general(
                    a, jnp.concatenate([b, turned], axis=1), (((0,), (0,)), ((), ())),
                    preferred_element_type=jnp.float32)
                ring[slot, 0, t] = both[:, :channels].astype(jnp.bfloat16)
                ring[slot, 1, t] = both[:, channels:].astype(jnp.bfloat16)

        @pl.when(jnp.logical_not(live))
        def _():
            ring[slot] = jnp.zeros(ring.shape[1:], jnp.bfloat16)

        copy(n).start()
        return 0

    total = owned * chunks
    lax.fori_loop(0, total, one, 0)
    for n in range(max(total - depth, 0), total):
        copy(n).wait()


def cross(sets, pairs, count, place, rows, owned):
    _, groups, bins, entries, channels = sets.shape
    step = math.gcd(bins, 8)
    smem = pl.BlockSpec(memory_space=pltpu.SMEM)
    return pl.pallas_call(
        functools.partial(cross_kernel, rows, owned),
        out_shape=jax.ShapeDtypeStruct(
            (1, 1, owned, 2, bins, channels, channels), jnp.bfloat16),
        in_specs=[smem, smem, smem, pl.BlockSpec(memory_space=pltpu.VMEM)],
        out_specs=pl.BlockSpec(memory_space=pl.ANY),
        scratch_shapes=[
            pltpu.VMEM((4, 2, step, channels, channels), jnp.bfloat16),
            pltpu.SemaphoreType.DMA((4,)),
        ],
        compiler_params=pltpu.CompilerParams(vmem_limit_bytes=40 * 2**20),
        cost_estimate=pl.CostEstimate(
            flops=4 * owned * bins * channels * channels * groups * entries,
            bytes_accessed=4 * owned * bins * channels * channels, transcendentals=0),
    )(pairs, count, place, sets)


def body(records, tile_pairs, tile_count, bin_index):
    rows, cols = lax.axis_size("row"), lax.axis_size("col")
    r, q = lax.axis_index("row"), lax.axis_index("col")
    sets = gather(records, dft_tables(bin_index, records.shape[2]), rows, cols)
    owned = tile_pairs.shape[2] // lax.axis_size("win")
    place = jnp.stack([lax.axis_index("win") * owned, r, q]).astype(jnp.int32)
    return cross(sets, jnp.swapaxes(tile_pairs, 2, 3), tile_count.reshape(-1), place, rows, owned)


def solution(mesh):
    return jax.shard_map(
        body,
        mesh=mesh,
        in_specs=(
            P("win", ("row", "col"), None),
            P("row", "col", None, None),
            P("row", "col"),
            P(),
        ),
        out_specs=P("row", "col", "win", None, None, None, None),
        check_vma=False,
    )
```

```python
import functools
import math

import jax
import jax.numpy as jnp
from jax import lax
from jax.experimental import pallas as pl
from jax.experimental.pallas import tpu as pltpu
from jax.sharding import PartitionSpec as P

GROUP = 8
UP, DOWN, PARTNER, RIGHT, LEFT, SIBLING = range(6)


def dft_tables(bin_index, length):
    sample_ids = jnp.arange(length, dtype=jnp.int32)
    phases = bin_index[:, None] * sample_ids[None, :] % length
    angles = 2.0 * math.pi / length * phases.astype(jnp.float32)
    window_taper = 0.5 - 0.5 * jnp.cos(2.0 * math.pi / length * sample_ids.astype(jnp.float32))
    cosine = window_taper[None, :] * jnp.cos(angles)
    sine = -window_taper[None, :] * jnp.sin(angles)
    return cosine.astype(jnp.bfloat16), sine.astype(jnp.bfloat16)


def gather_kernel(rows, cols, groups, rec_hbm, cos_ref, sin_ref, sets, rec, spec, own,
                  rec_sem, local_sem, send_sem, recv_sem):
    w, r, q = lax.axis_index("win"), lax.axis_index("row"), lax.axis_index("col")
    chips = cols // 2
    x = q // 2
    other = 1 - w
    sib = q + 1 - 2 * (q % 2)
    mine, theirs = w * groups, other * groups
    device = {
        UP: (w, r + 1, q), DOWN: (w, r - 1, q), PARTNER: (other, r, q),
        RIGHT: (w, r, q + 2), LEFT: (w, r, q - 2), SIBLING: (w, r, sib),
    }
    exists = {
        UP: r < rows - 1, DOWN: r > 0, PARTNER: None,
        RIGHT: x < chips - 1, LEFT: x > 0, SIBLING: None,
    }

    def fetch(i):
        part = pl.ds(i * GROUP, GROUP)
        return pltpu.make_async_copy(rec_hbm.at[part], rec.at[part], rec_sem.at[i])

    for i in range(groups):
        fetch(i).start()

    def guarded(way, f):
        if exists[way] is None:
            f()
        else:
            pl.when(exists[way])(f)

    barrier = pltpu.get_barrier_semaphore()
    for way in range(6):
        guarded(way, lambda way=way: pl.semaphore_signal(
            barrier, inc=1, device_id=device[way], device_id_type=pl.DeviceIdType.MESH))
    ends = sum(exists[way].astype(jnp.int32) for way in (UP, DOWN, RIGHT, LEFT))

    def copy(way, src, slot, g):
        return pltpu.make_async_remote_copy(
            src_ref=src, dst_ref=sets.at[slot, g], send_sem=send_sem.at[way, slot, g],
            recv_sem=recv_sem.at[slot, g], device_id=device[way],
            device_id_type=pl.DeviceIdType.MESH)

    pending = []

    def send(way, src, slot, g, cond=None):
        def go():
            guarded(way, lambda: copy(way, src, slot, g).start())

        def done():
            guarded(way, lambda: copy(way, src, slot, g).wait_send())

        if cond is None:
            go()
        pending.append((cond, done))
        return go

    def arrived(slot, g):
        copy(PARTNER, sets.at[slot, g], slot, g).wait_recv()

    bins = cos_ref.shape[0]
    keeps = []
    for i in range(groups):
        fetch(i).wait()

        def one_window(v, _, i=i):
            table = jnp.concatenate([cos_ref[...], sin_ref[...]], axis=0)
            s = lax.dot_general(table, rec[i * GROUP + v], (((1,), (1,)), ((), ())),
                                preferred_element_type=jnp.float32)
            scale = 1.0 / jnp.sqrt(jnp.mean(s * s, axis=0, keepdims=True) + 1e-06)
            s = s * scale
            for lane in range(spec.shape[0]):
                part = s[:, lane * 128:(lane + 1) * 128]
                spec[lane, pl.ds(v, bins, stride=2 * GROUP), :] = part[:bins]
                spec[lane, pl.ds(v + GROUP, bins, stride=2 * GROUP), :] = part[bins:]
            return 0

        lax.fori_loop(0, GROUP, one_window, 0, unroll=4)
        for lane in range(spec.shape[0]):
            own[i, :, :, lane * 128:(lane + 1) * 128] = spec[lane].astype(jnp.bfloat16).reshape(
                own.shape[1], own.shape[2], 128)
        if i == 0:
            pl.semaphore_wait(barrier, 2 + ends)
        for way in (UP, DOWN, PARTNER):
            send(way, own.at[i], r, mine + i)
        for way in (RIGHT, LEFT, SIBLING):
            send(way, own.at[i], rows + q, mine + i)
        keep = pltpu.make_async_copy(own.at[i], sets.at[r, mine + i], local_sem.at[i])
        keep.start()
        keeps.append(keep)

    def relay(cond, slot, g, ways):
        goes = [send(way, sets.at[slot, g], slot, g, cond) for way in ways]

        def go():
            arrived(slot, g)
            for f in goes:
                f()

        pl.when(cond)(go)

    def along_x(g):
        for d in range(1, chips):
            relay(x - d >= 0, rows + q - 2 * d, g, (RIGHT, SIBLING))
            relay(x + d < chips, rows + q + 2 * d, g, (LEFT, SIBLING))

    def extra(up, down):
        g = theirs + groups - 1
        for way, cond in ((UP, up), (DOWN, down)):
            pl.when(cond)(send(way, sets.at[r, g], r, g, cond))

    for h in range(1, rows):
        for i in range(groups):
            shared = () if h == 1 and i == groups - 1 else (PARTNER,)
            relay(r - h >= 0, r - h, mine + i, (UP,) + shared)
            relay(r + h < rows, r + h, mine + i, (DOWN,) + shared)
            if h == 1:
                arrived(r, theirs + i)
                for way in (RIGHT, LEFT, SIBLING):
                    send(way, sets.at[r, theirs + i], rows + q, theirs + i)
            if h == 1 and i == groups - 1:
                extra(r < rows - 2, r > 1)
        if h == 1:
            for i in range(groups):
                along_x(mine + i)
        if h == max(1, rows - 2):
            for i in range(groups):
                along_x(theirs + i)
    extra(r == rows - 2, r == 1)

    for h in range(1, rows):
        for i in range(groups):
            pl.when(r - h >= 0)(lambda h=h, i=i: arrived(r - h, theirs + i))
            pl.when(r + h < rows)(lambda h=h, i=i: arrived(r + h, theirs + i))
    for c in range(chips):
        for g in range(2 * groups):
            arrived(rows + 2 * c + 1 - q % 2, g)
    for keep in keeps:
        keep.wait()
    for cond, done in pending:
        if cond is None:
            done()
        else:
            pl.when(cond)(done)


def gather(records, tables, rows, cols):
    windows, channels, length = records.shape
    groups = windows // GROUP
    entries = 2 * tables[0].shape[0]
    bins = entries // 2
    slots = rows + cols
    return pl.pallas_call(
        functools.partial(gather_kernel, rows, cols, groups),
        out_shape=jax.ShapeDtypeStruct(
            (slots, 2 * groups, bins, 2 * GROUP, channels), jnp.bfloat16),
        in_specs=[pl.BlockSpec(memory_space=pl.ANY)] + [pl.BlockSpec(memory_space=pltpu.VMEM)] * 2,
        out_specs=pl.BlockSpec(memory_space=pl.ANY),
        scratch_shapes=[
            pltpu.VMEM(records.shape, jnp.bfloat16),
            pltpu.VMEM((channels // 128, entries * GROUP, 128), jnp.float32),
            pltpu.VMEM((groups, bins, 2 * GROUP, channels), jnp.bfloat16),
            pltpu.SemaphoreType.DMA((groups,)),
            pltpu.SemaphoreType.DMA((groups,)),
            pltpu.SemaphoreType.DMA((6, slots, 2 * groups)),
            pltpu.SemaphoreType.DMA((slots, 2 * groups)),
        ],
        compiler_params=pltpu.CompilerParams(
            collective_id=0, has_side_effects=True, vmem_limit_bytes=40 * 2**20),
        cost_estimate=pl.CostEstimate(
            flops=2 * windows * channels * length * entries,
            bytes_accessed=windows * channels * length * 2, transcendentals=0),
    )(records, *tables)


def cross_kernel(rows, owned, pairs, count, place, sets, out, ring, sem):
    depth, _, step, channels, _ = ring.shape
    groups = sets.shape[1]
    chunks = out.shape[4] // step

    def copy(n):
        part = pl.ds((n % chunks) * step, step)
        return pltpu.make_async_copy(
            ring.at[n % depth], out.at[0, 0, n // chunks, :, part], sem.at[n % depth])

    def one(n, _):
        slot = n % depth
        position = place[0] + n // chunks
        i, j = pairs[0, 0, 0, position], pairs[0, 0, 1, position]
        first = jnp.where(i == place[2], place[1], rows + i)
        live = position < count[0]

        @pl.when(n >= depth)
        def _():
            copy(n - depth).wait()

        @pl.when(live)
        def _():
            for t in range(step):
                k = (n % chunks) * step + t
                a = sets[first, :, k].reshape(-1, channels)
                b = sets[j, :, k].reshape(a.shape)
                parts = b.astype(jnp.float32).reshape(groups, 2, GROUP, channels)
                turned = jnp.concatenate([-parts[:, 1:], parts[:, :1]], axis=1)
                turned = turned.reshape(a.shape).astype(jnp.bfloat16)
                both = lax.dot_general(
                    a, jnp.concatenate([b, turned], axis=1), (((0,), (0,)), ((), ())),
                    preferred_element_type=jnp.float32)
                ring[slot, 0, t] = both[:, :channels].astype(jnp.bfloat16)
                ring[slot, 1, t] = both[:, channels:].astype(jnp.bfloat16)

        @pl.when(jnp.logical_not(live))
        def _():
            ring[slot] = jnp.zeros(ring.shape[1:], jnp.bfloat16)

        copy(n).start()
        return 0

    total = owned * chunks
    lax.fori_loop(0, total, one, 0)
    for n in range(max(total - depth, 0), total):
        copy(n).wait()


def cross(sets, pairs, count, place, rows, owned):
    _, groups, bins, entries, channels = sets.shape
    step = math.gcd(bins, 8)
    smem = pl.BlockSpec(memory_space=pltpu.SMEM)
    return pl.pallas_call(
        functools.partial(cross_kernel, rows, owned),
        out_shape=jax.ShapeDtypeStruct(
            (1, 1, owned, 2, bins, channels, channels), jnp.bfloat16),
        in_specs=[smem, smem, smem, pl.BlockSpec(memory_space=pltpu.VMEM)],
        out_specs=pl.BlockSpec(memory_space=pl.ANY),
        scratch_shapes=[
            pltpu.VMEM((4, 2, step, channels, channels), jnp.bfloat16),
            pltpu.SemaphoreType.DMA((4,)),
        ],
        compiler_params=pltpu.CompilerParams(vmem_limit_bytes=40 * 2**20),
        cost_estimate=pl.CostEstimate(
            flops=4 * owned * bins * channels * channels * groups * entries,
            bytes_accessed=4 * owned * bins * channels * channels, transcendentals=0),
    )(pairs, count, place, sets)


def body(records, tile_pairs, tile_count, bin_index):
    rows, cols = lax.axis_size("row"), lax.axis_size("col")
    r, q = lax.axis_index("row"), lax.axis_index("col")
    sets = gather(records, dft_tables(bin_index, records.shape[2]), rows, cols)
    owned = tile_pairs.shape[2] // lax.axis_size("win")
    place = jnp.stack([lax.axis_index("win") * owned, r, q]).astype(jnp.int32)
    return cross(sets, jnp.swapaxes(tile_pairs, 2, 3), tile_count.reshape(-1), place, rows, owned)


def solution(mesh):
    return jax.shard_map(
        body,
        mesh=mesh,
        in_specs=(
            P("win", ("row", "col"), None),
            P("row", "col", None, None),
            P("row", "col"),
            P(),
        ),
        out_specs=P("row", "col", "win", None, None, None, None),
        check_vma=False,
    )
```

```python
import functools
import math

import jax
import jax.numpy as jnp
from jax import lax
from jax.experimental import pallas as pl
from jax.experimental.pallas import tpu as pltpu
from jax.sharding import PartitionSpec as P

GROUP = 8
UP, DOWN, PARTNER, RIGHT, LEFT, SIBLING = range(6)


def dft_tables(bin_index, length):
    sample_ids = jnp.arange(length, dtype=jnp.int32)
    phases = bin_index[:, None] * sample_ids[None, :] % length
    angles = 2.0 * math.pi / length * phases.astype(jnp.float32)
    window_taper = 0.5 - 0.5 * jnp.cos(2.0 * math.pi / length * sample_ids.astype(jnp.float32))
    cosine = window_taper[None, :] * jnp.cos(angles)
    sine = -window_taper[None, :] * jnp.sin(angles)
    return cosine.astype(jnp.bfloat16), sine.astype(jnp.bfloat16)


def gather_kernel(rows, cols, groups, rec_hbm, cos_ref, sin_ref, sets, rec, spec, own,
                  rec_sem, local_sem, send_sem, recv_sem):
    w, r, q = lax.axis_index("win"), lax.axis_index("row"), lax.axis_index("col")
    chips = cols // 2
    x = q // 2
    other = 1 - w
    sib = q + 1 - 2 * (q % 2)
    mine, theirs = w * groups, other * groups
    device = {
        UP: (w, r + 1, q), DOWN: (w, r - 1, q), PARTNER: (other, r, q),
        RIGHT: (w, r, q + 2), LEFT: (w, r, q - 2), SIBLING: (w, r, sib),
    }
    exists = {
        UP: r < rows - 1, DOWN: r > 0, PARTNER: None,
        RIGHT: x < chips - 1, LEFT: x > 0, SIBLING: None,
    }

    def fetch(i):
        part = pl.ds(i * GROUP, GROUP)
        return pltpu.make_async_copy(rec_hbm.at[part], rec.at[part], rec_sem.at[i])

    for i in range(groups):
        fetch(i).start()

    def guarded(way, f):
        if exists[way] is None:
            f()
        else:
            pl.when(exists[way])(f)

    barrier = pltpu.get_barrier_semaphore()
    for way in range(6):
        guarded(way, lambda way=way: pl.semaphore_signal(
            barrier, inc=1, device_id=device[way], device_id_type=pl.DeviceIdType.MESH))
    ends = sum(exists[way].astype(jnp.int32) for way in (UP, DOWN, RIGHT, LEFT))

    def copy(way, src, slot, g):
        return pltpu.make_async_remote_copy(
            src_ref=src, dst_ref=sets.at[slot, g], send_sem=send_sem.at[way, slot, g],
            recv_sem=recv_sem.at[slot, g], device_id=device[way],
            device_id_type=pl.DeviceIdType.MESH)

    pending = []

    def send(way, src, slot, g, cond=None):
        def go():
            guarded(way, lambda: copy(way, src, slot, g).start())

        def done():
            guarded(way, lambda: copy(way, src, slot, g).wait_send())

        if cond is None:
            go()
        pending.append((cond, done))
        return go

    def arrived(slot, g):
        copy(PARTNER, sets.at[slot, g], slot, g).wait_recv()

    bins = cos_ref.shape[0]
    keeps = []
    for i in range(groups):
        fetch(i).wait()

        def one_window(v, _, i=i):
            table = jnp.concatenate([cos_ref[...], sin_ref[...]], axis=0)
            s = lax.dot_general(table, rec[i * GROUP + v], (((1,), (1,)), ((), ())),
                                preferred_element_type=jnp.float32)
            scale = 1.0 / jnp.sqrt(jnp.mean(s * s, axis=0, keepdims=True) + 1e-06)
            s = s * scale
            for lane in range(spec.shape[0]):
                part = s[:, lane * 128:(lane + 1) * 128]
                spec[lane, pl.ds(v, bins, stride=2 * GROUP), :] = part[:bins]
                spec[lane, pl.ds(v + GROUP, bins, stride=2 * GROUP), :] = part[bins:]
            return 0

        lax.fori_loop(0, GROUP, one_window, 0, unroll=4)
        for lane in range(spec.shape[0]):
            own[i, :, :, lane * 128:(lane + 1) * 128] = spec[lane].astype(jnp.bfloat16).reshape(
                own.shape[1], own.shape[2], 128)
        if i == 0:
            pl.semaphore_wait(barrier, 2 + ends)
        for way in (UP, DOWN, PARTNER):
            send(way, own.at[i], r, mine + i)
        for way in (RIGHT, LEFT, SIBLING):
            send(way, own.at[i], rows + q, mine + i)
        keep = pltpu.make_async_copy(own.at[i], sets.at[r, mine + i], local_sem.at[i])
        keep.start()
        keeps.append(keep)

    def relay(cond, slot, g, ways):
        goes = [send(way, sets.at[slot, g], slot, g, cond) for way in ways]

        def go():
            arrived(slot, g)
            for f in goes:
                f()

        pl.when(cond)(go)

    def along_x(g):
        for d in range(1, chips):
            relay(x - d >= 0, rows + q - 2 * d, g, (RIGHT, SIBLING))
            relay(x + d < chips, rows + q + 2 * d, g, (LEFT, SIBLING))

    def extra(up, down):
        g = theirs + groups - 1
        for way, cond in ((UP, up), (DOWN, down)):
            pl.when(cond)(send(way, sets.at[r, g], r, g, cond))

    for h in range(1, rows):
        for i in range(groups):
            shared = () if h == 1 and i == groups - 1 else (PARTNER,)
            relay(r - h >= 0, r - h, mine + i, (UP,) + shared)
            relay(r + h < rows, r + h, mine + i, (DOWN,) + shared)
            if h == 1:
                arrived(r, theirs + i)
                for way in (RIGHT, LEFT, SIBLING):
                    send(way, sets.at[r, theirs + i], rows + q, theirs + i)
            if h == 1 and i == groups - 1:
                extra(r < rows - 2, r > 1)
        if h == max(1, rows - 2):
            for i in range(groups):
                along_x(mine + i)
    for i in range(groups):
        along_x(theirs + i)
    extra(r == rows - 2, r == 1)

    for h in range(1, rows):
        for i in range(groups):
            pl.when(r - h >= 0)(lambda h=h, i=i: arrived(r - h, theirs + i))
            pl.when(r + h < rows)(lambda h=h, i=i: arrived(r + h, theirs + i))
    for c in range(chips):
        for g in range(2 * groups):
            arrived(rows + 2 * c + 1 - q % 2, g)
    for keep in keeps:
        keep.wait()
    for cond, done in pending:
        if cond is None:
            done()
        else:
            pl.when(cond)(done)


def gather(records, tables, rows, cols):
    windows, channels, length = records.shape
    groups = windows // GROUP
    entries = 2 * tables[0].shape[0]
    bins = entries // 2
    slots = rows + cols
    return pl.pallas_call(
        functools.partial(gather_kernel, rows, cols, groups),
        out_shape=jax.ShapeDtypeStruct(
            (slots, 2 * groups, bins, 2 * GROUP, channels), jnp.bfloat16),
        in_specs=[pl.BlockSpec(memory_space=pl.ANY)] + [pl.BlockSpec(memory_space=pltpu.VMEM)] * 2,
        out_specs=pl.BlockSpec(memory_space=pl.ANY),
        scratch_shapes=[
            pltpu.VMEM(records.shape, jnp.bfloat16),
            pltpu.VMEM((channels // 128, entries * GROUP, 128), jnp.float32),
            pltpu.VMEM((groups, bins, 2 * GROUP, channels), jnp.bfloat16),
            pltpu.SemaphoreType.DMA((groups,)),
            pltpu.SemaphoreType.DMA((groups,)),
            pltpu.SemaphoreType.DMA((6, slots, 2 * groups)),
            pltpu.SemaphoreType.DMA((slots, 2 * groups)),
        ],
        compiler_params=pltpu.CompilerParams(
            collective_id=0, has_side_effects=True, vmem_limit_bytes=40 * 2**20),
        cost_estimate=pl.CostEstimate(
            flops=2 * windows * channels * length * entries,
            bytes_accessed=windows * channels * length * 2, transcendentals=0),
    )(records, *tables)


def cross_kernel(rows, owned, pairs, count, place, sets, out, ring, sem):
    depth, _, step, channels, _ = ring.shape
    groups = sets.shape[1]
    chunks = out.shape[4] // step

    def copy(n):
        part = pl.ds((n % chunks) * step, step)
        return pltpu.make_async_copy(
            ring.at[n % depth], out.at[0, 0, n // chunks, :, part], sem.at[n % depth])

    def one(n, _):
        slot = n % depth
        position = place[0] + n // chunks
        i, j = pairs[0, 0, 0, position], pairs[0, 0, 1, position]
        first = jnp.where(i == place[2], place[1], rows + i)
        live = position < count[0]

        @pl.when(n >= depth)
        def _():
            copy(n - depth).wait()

        @pl.when(live)
        def _():
            for t in range(step):
                k = (n % chunks) * step + t
                a = sets[first, :, k].reshape(-1, channels)
                b = sets[j, :, k].reshape(a.shape)
                parts = b.astype(jnp.float32).reshape(groups, 2, GROUP, channels)
                turned = jnp.concatenate([-parts[:, 1:], parts[:, :1]], axis=1)
                turned = turned.reshape(a.shape).astype(jnp.bfloat16)
                both = lax.dot_general(
                    a, jnp.concatenate([b, turned], axis=1), (((0,), (0,)), ((), ())),
                    preferred_element_type=jnp.float32)
                ring[slot, 0, t] = both[:, :channels].astype(jnp.bfloat16)
                ring[slot, 1, t] = both[:, channels:].astype(jnp.bfloat16)

        @pl.when(jnp.logical_not(live))
        def _():
            ring[slot] = jnp.zeros(ring.shape[1:], jnp.bfloat16)

        copy(n).start()
        return 0

    total = owned * chunks
    lax.fori_loop(0, total, one, 0)
    for n in range(max(total - depth, 0), total):
        copy(n).wait()


def cross(sets, pairs, count, place, rows, owned):
    _, groups, bins, entries, channels = sets.shape
    step = math.gcd(bins, 8)
    smem = pl.BlockSpec(memory_space=pltpu.SMEM)
    return pl.pallas_call(
        functools.partial(cross_kernel, rows, owned),
        out_shape=jax.ShapeDtypeStruct(
            (1, 1, owned, 2, bins, channels, channels), jnp.bfloat16),
        in_specs=[smem, smem, smem, pl.BlockSpec(memory_space=pltpu.VMEM)],
        out_specs=pl.BlockSpec(memory_space=pl.ANY),
        scratch_shapes=[
            pltpu.VMEM((4, 2, step, channels, channels), jnp.bfloat16),
            pltpu.SemaphoreType.DMA((4,)),
        ],
        compiler_params=pltpu.CompilerParams(vmem_limit_bytes=40 * 2**20),
        cost_estimate=pl.CostEstimate(
            flops=4 * owned * bins * channels * channels * groups * entries,
            bytes_accessed=4 * owned * bins * channels * channels, transcendentals=0),
    )(pairs, count, place, sets)


def body(records, tile_pairs, tile_count, bin_index):
    rows, cols = lax.axis_size("row"), lax.axis_size("col")
    r, q = lax.axis_index("row"), lax.axis_index("col")
    sets = gather(records, dft_tables(bin_index, records.shape[2]), rows, cols)
    owned = tile_pairs.shape[2] // lax.axis_size("win")
    place = jnp.stack([lax.axis_index("win") * owned, r, q]).astype(jnp.int32)
    return cross(sets, jnp.swapaxes(tile_pairs, 2, 3), tile_count.reshape(-1), place, rows, owned)


def solution(mesh):
    return jax.shard_map(
        body,
        mesh=mesh,
        in_specs=(
            P("win", ("row", "col"), None),
            P("row", "col", None, None),
            P("row", "col"),
            P(),
        ),
        out_specs=P("row", "col", "win", None, None, None, None),
        check_vma=False,
    )
```
